32 devices in a mesh: layer: 4 (over y, x), feat: 8 (over z, core).
Axes of the slice: x: 2, y: 2, z: 4, core: 2. Of those that a mesh axis runs over, the one named last changes fastest.
Arguments:
- inputs: bfloat16 [4, 512, 2048], P('layer', 'feat'), may hold values from -6 to 6
- targets: bfloat16 [4, 512, 2048], P('layer', 'feat'), may hold values from -6 to 6
- enc_weight: bfloat16 [4, 2048, 16384], P('layer', None, 'feat'), may hold values from -0.125 to 0.125
- enc_bias: float32 [4, 16384], P('layer', 'feat'), may hold values from -1 to 0.5
- dec_weight: bfloat16 [4, 2, 16384, 2048], P('layer', None, 'feat'), may hold values from -0.046875 to 0.046875
- dec_bias: float32 [4, 2048], P('layer'), may hold values from -3 to 3
Outputs:
- mean_loss: float32 [], replicated
- enc_grad: bfloat16 [4, 2048, 16384], P('layer', None, 'feat')
- enc_bias_grad: float32 [4, 16384], P('layer', 'feat')
- dec_grad: bfloat16 [4, 2, 16384, 2048], P('layer', None, 'feat')
- dec_bias_grad: float32 [4, 2048], P('layer')
The draws below stay inside these ranges and needn't reach their ends.
All inputs are finite; a program needn't handle non-finite values.
Results may differ from the reference program's by a relative error of at most 0.006.
Values may be sent and summed in bfloat16 or wider, within the bound.
No kernel may reach another device: no remote copies, remote signals or barrier semaphores. Data moves between devices by JAX's collectives and lax.ppermute only.
A program may use at most 128 MiB of HBM per device.

```python
import jax
import jax.numpy as jnp

D = 2048
FEATURES = 16384
REACH = 2
TOKENS = 512
LAYERS = 4


def steps_of(rng, extent, split, smallest, top_value):
    gain = 1.0
    for axis_at, parts in split:
        steps = jax.random.uniform(jax.random.fold_in(jax.random.fold_in(rng, 6), axis_at), (parts,), jnp.float32, smallest / len(split), top_value / len(split))
        gain = gain * jnp.repeat(jnp.exp(steps), extent[axis_at] // parts).reshape((-1,) + (1,) * (len(extent) - 1 - axis_at))
    return gain


def scatter_about(rng, shape, width, reach, cuts=(), kind=jnp.bfloat16):
    loudness = steps_of(rng, shape, cuts, -0.22, 0.18) if cuts else 1.0
    result = jax.random.normal(rng, shape, jnp.float32) * width * loudness
    return jnp.minimum(jnp.maximum(result, -reach), reach).astype(kind)


def setup_inputs(seed: int = 0) -> dict:
    keys = jax.random.split(jax.random.key(seed), 7)
    return {
        "inputs": scatter_about(keys[0], (LAYERS, TOKENS, D), 1.0, 6.0, ((0, 4), (1, 8))),
        "targets": scatter_about(keys[1], (LAYERS, TOKENS, D), 1.0, 6.0, ((0, 4), (1, 8))),
        "enc_weight": scatter_about(keys[2], (LAYERS, D, FEATURES), D ** -0.5, 0.125, ((0, 4), (2, 8))),
        "enc_bias": jnp.clip(-1.0 + 1.5 * jax.random.uniform(keys[3], (LAYERS, FEATURES), jnp.float32) ** steps_of(keys[3], (LAYERS, FEATURES), ((0, 4), (1, 8)), -0.2, 0.2), -1.0, 0.5),
        "dec_weight": scatter_about(keys[4], (LAYERS, REACH, FEATURES, D), FEATURES ** -0.5, 0.046875, ((0, 4), (2, 8))),
        "dec_bias": scatter_about(keys[5], (LAYERS, D), 0.5, 3.0, ((0, 4),), jnp.float32),
    }


def reference(inputs, targets, enc_weight, enc_bias, dec_weight, dec_bias):
    pres = []
    acts = []
    for layer_idx in range(LAYERS):
        pre = jnp.dot(inputs[layer_idx], enc_weight[layer_idx], preferred_element_type=jnp.float32) + enc_bias[layer_idx]
        pres.append(pre)
        acts.append((jnp.maximum(pre, 0.0) ** 2).astype(jnp.bfloat16))
    grads = []
    for target_idx in range(LAYERS):
        recon = dec_bias[target_idx].astype(jnp.float32)
        for offset in range(REACH):
            source = target_idx - offset
            if source >= 0:
                recon = recon + jnp.dot(acts[source], dec_weight[source, offset], preferred_element_type=jnp.float32)
        grads.append((recon - targets[target_idx].astype(jnp.float32)).astype(jnp.bfloat16))
    total = jnp.float32(0.0)
    for target_idx in range(LAYERS):
        total = total + jnp.sum(grads[target_idx].astype(jnp.float32) ** 2)
    mean_loss = total / (LAYERS * TOKENS * D)
    enc_grads = []
    enc_bias_grads = []
    dec_grads = []
    dec_bias_grads = []
    for layer_idx in range(LAYERS):
        back = jnp.zeros((TOKENS, FEATURES), jnp.float32)
        per_reach = []
        for offset in range(REACH):
            target_idx = layer_idx + offset
            if target_idx < LAYERS:
                per_reach.append(jnp.dot(acts[layer_idx].T, grads[target_idx], preferred_element_type=jnp.float32).astype(jnp.bfloat16))
                back = back + jnp.dot(grads[target_idx], dec_weight[layer_idx, offset].T, preferred_element_type=jnp.float32)
            else:
                per_reach.append(jnp.zeros((FEATURES, D), jnp.bfloat16))
        dec_grads.append(jnp.stack(per_reach, axis=0))
        dpre = (back * 2.0 * jnp.maximum(pres[layer_idx], 0.0)).astype(jnp.bfloat16)
        enc_grads.append(jnp.dot(inputs[layer_idx].T, dpre, preferred_element_type=jnp.float32).astype(jnp.bfloat16))
        enc_bias_grads.append(jnp.sum(dpre.astype(jnp.float32), axis=0))
        dec_bias_grads.append(jnp.sum(grads[layer_idx].astype(jnp.float32), axis=0))
    return (mean_loss, jnp.stack(enc_grads, 0), jnp.stack(enc_bias_grads, 0), jnp.stack(dec_grads, 0), jnp.stack(dec_bias_grads, 0))
```

```python
import jax
import jax.numpy as jnp
from jax import lax
from jax.sharding import PartitionSpec as P


def swapped(block):
    size = lax.axis_size("feat")
    return lax.ppermute(block, "feat", [(i, i ^ 1) for i in range(size)])


def from_below(block):
    size = lax.axis_size("feat")
    return lax.ppermute(block, "feat", [(i, (i + 2) % size) for i in range(size)])


def from_layer(block, distance):
    layers = range(lax.axis_size("layer"))
    return lax.ppermute(block, "layer", [(i, i + distance) for i in layers if i + distance in layers])


def shards(inputs, targets, enc_weight, enc_bias, dec_weight, dec_bias):
    rows = inputs.shape[1]
    width = dec_weight.shape[3]
    chips = lax.axis_size("feat") // 2
    f32, bf16 = jnp.float32, jnp.bfloat16

    tokens = [None] * chips
    held = inputs[0]
    for j in range(chips):
        tokens[j] = jnp.concatenate([held, swapped(held)], axis=0)
        if j < chips - 1:
            held = from_below(held)

    pres, acts, sums = [None] * chips, [None] * chips, [None] * chips
    for j in list(range(1, chips)) + [0]:
        pre = jnp.dot(tokens[j], enc_weight[0], preferred_element_type=f32) + enc_bias[0]
        pres[j] = jnp.maximum(pre, 0.0)
        acts[j] = (pres[j] ** 2).astype(bf16)
        here = jnp.dot(acts[j], dec_weight[0, 0], preferred_element_type=f32)
        later = jnp.dot(acts[j], dec_weight[0, 1], preferred_element_type=f32)
        here_sum = here[:rows] + swapped(here[rows:].astype(bf16)).astype(f32)
        later_sum = later[:rows] + swapped(later[rows:].astype(bf16)).astype(f32)
        sums[j] = here_sum + from_layer(later_sum.astype(bf16), 1).astype(f32)

    total = sums[1 % chips]
    for j in list(range(2, chips)) + [0]:
        if chips > 1:
            total = from_below(total.astype(bf16)).astype(f32) + sums[j]

    grad = (total + dec_bias[0] - targets[0].astype(f32)).astype(bf16)
    squares = lax.psum(jnp.sum(grad.astype(f32) ** 2), ("layer", "feat"))
    mean_loss = squares / (lax.axis_size("layer") * lax.axis_size("feat") * rows * width)

    heres, laters, dpres = [], [], []
    held = grad
    for j in range(chips):
        ahead = from_layer(held, -1)
        here = jnp.concatenate([held, swapped(held)], axis=0)
        later = jnp.concatenate([ahead, swapped(ahead)], axis=0)
        if j < chips - 1:
            held = from_below(held)
        back = jnp.einsum("td,fd->tf", here, dec_weight[0, 0], preferred_element_type=f32)
        back = back + jnp.einsum("td,fd->tf", later, dec_weight[0, 1], preferred_element_type=f32)
        dpres.append((back * 2.0 * pres[j]).astype(bf16))
        heres.append(here)
        laters.append(later)

    here, later = jnp.concatenate(heres, 0), jnp.concatenate(laters, 0)
    dpre, act, token = jnp.concatenate(dpres, 0), jnp.concatenate(acts, 0), jnp.concatenate(tokens, 0)
    dec_grad = jnp.stack(
        [jnp.einsum("tf,td->fd", act, g, preferred_element_type=f32).astype(bf16) for g in (here, later)]
    )
    enc_grad = jnp.einsum("td,tf->df", token, dpre, preferred_element_type=f32).astype(bf16)
    enc_bias_grad = jnp.sum(dpre.astype(f32), axis=0)
    dec_bias_grad = jnp.sum(here.astype(f32), axis=0)
    return (mean_loss, enc_grad[None], enc_bias_grad[None], dec_grad[None], dec_bias_grad[None])


def solution(mesh):
    return jax.shard_map(
        shards,
        mesh=mesh,
        in_specs=(
            P("layer", "feat", None),
            P("layer", "feat", None),
            P("layer", None, "feat"),
            P("layer", "feat"),
            P("layer", None, "feat", None),
            P("layer", None),
        ),
        out_specs=(
            P(),
            P("layer", None, "feat"),
            P("layer", "feat"),
            P("layer", None, "feat", None),
            P("layer", None),
        ),
        check_vma=False,
    )
```

```python
import math

import jax
import jax.numpy as jnp
from jax import lax
from jax.experimental import pallas as pl
from jax.experimental.pallas import tpu as pltpu
from jax.sharding import PartitionSpec as P

f32, bf16 = jnp.float32, jnp.bfloat16
MIB = 2**20
VMEM = pl.BlockSpec(memory_space=pltpu.VMEM)
HBM = pl.BlockSpec(memory_space=pltpu.HBM)
ANY = pl.BlockSpec(memory_space=pl.ANY)


def swapped(block):
    size = lax.axis_size("feat")
    return lax.ppermute(block, "feat", [(i, i ^ 1) for i in range(size)])


def from_below(block, distance=1):
    size = lax.axis_size("feat")
    return lax.ppermute(block, "feat", [(i, (i + 2 * distance) % size) for i in range(size)])


def round_layers(block, distance):
    size = lax.axis_size("layer")
    return lax.ppermute(block, "layer", [(i, (i + distance) % size) for i in range(size)])


def after(value, *others):
    return lax.optimization_barrier((value, *others))[0]


def shape(dims, dtype):
    return jax.ShapeDtypeStruct(dims, dtype)


def call(name, kernel, flops, args, out_shape, limit, in_specs=None, out_specs=None, scratch=(), aliases=None):
    size = sum(math.prod(a.shape) * jnp.dtype(a.dtype).itemsize for a in (*args, *out_shape))
    return pl.pallas_call(
        kernel,
        in_specs=in_specs or [VMEM] * len(args),
        out_specs=out_specs or [VMEM] * len(out_shape),
        out_shape=out_shape,
        scratch_shapes=scratch,
        input_output_aliases=aliases or {},
        name=name,
        compiler_params=pltpu.CompilerParams(vmem_limit_bytes=limit * MIB),
        cost_estimate=pl.CostEstimate(flops=flops, bytes_accessed=size, transcendentals=0),
    )(*args)


def stacked(refs, at=slice(None)):
    return jnp.concatenate([ref[:, at] for ref in refs], axis=0)


def column_sums(values):
    return jnp.sum(values, axis=0, keepdims=True)


def over_tiles(size, body):
    tile = min(512, size)

    @pl.loop(0, size // tile)
    def _(i):
        body(pl.ds(pl.multiple_of(i * tile, tile), tile))


def encode(token, weight_ref, bias_ref, pre_ref, act_ref):
    def body(at):
        pre = jnp.dot(token, weight_ref[:, at], preferred_element_type=f32) + bias_ref[:, at]
        pre = jnp.maximum(pre, 0.0)
        pre_ref[:, at] = pre
        act_ref[:, at] = (pre * pre).astype(bf16)

    over_tiles(weight_ref.shape[1], body)


def decode(act_ref, weight_refs, mine_ref, theirs_ref):
    rows = mine_ref.shape[0]
    width = weight_refs[0].shape[1]
    tile = min(512, width)
    for k, weight_ref in enumerate(weight_refs):

        @pl.loop(0, width // tile)
        def _(i, k=k, weight_ref=weight_ref):
            at = pl.ds(pl.multiple_of(i * tile, tile), tile)
            to = pl.ds(pl.multiple_of(k * width + i * tile, tile), tile)
            out = jnp.dot(act_ref[...], weight_ref[:, at], preferred_element_type=f32)
            mine_ref[:, to] = out[:rows]
            theirs_ref[:, to] = out[rows:].astype(bf16)


def first_back(grad_refs, weight_ref, entries, back_ref, sum_ref, square_ref):
    grad = stacked(grad_refs)
    wide = grad.astype(f32)
    sum_ref[...] = column_sums(wide)
    square_ref[...] = column_sums(wide * wide) / entries

    def body(at):
        back_ref[:, at] = jnp.dot(grad, weight_ref[:, at], preferred_element_type=f32)

    over_tiles(weight_ref.shape[1], body)


def second_back(grad_refs, weight_ref, back_ref, pre_ref, dpre_ref, sum_ref):
    grad = stacked(grad_refs)

    def body(at):
        out = back_ref[:, at] + jnp.dot(grad, weight_ref[:, at], preferred_element_type=f32)
        dpre = (out * 2.0 * pre_ref[:, at]).astype(bf16)
        dpre_ref[:, at] = dpre
        sum_ref[:, at] = column_sums(dpre.astype(f32))

    over_tiles(weight_ref.shape[1], body)


def outers(jobs, buffer_ref, sem_ref):
    copies = []
    for left_refs, right_refs, out_ref in jobs:
        rows, columns = out_ref.shape
        high, wide = min(512, rows), min(512, columns)
        for start in range(0, rows, high):
            slot = len(copies) % 2
            if len(copies) >= 2:
                copies[-2].wait()
            turned = stacked(left_refs, pl.ds(start, high)).T
            for at in range(0, columns, wide):
                at = pl.ds(at, wide)
                out = jnp.dot(turned, stacked(right_refs, at), preferred_element_type=f32)
                buffer_ref[slot, :high, at] = out.astype(bf16)
            source = buffer_ref.at[slot, :high, :columns]
            copy = pltpu.make_async_copy(source, out_ref.at[pl.ds(start, high)], sem_ref.at[slot])
            copy.start()
            copies.append(copy)
    for copy in copies[-2:]:
        copy.wait()


def outer_scratch(rows, columns):
    return [pltpu.VMEM((2, min(512, rows), columns), bf16), pltpu.SemaphoreType.DMA((2,))]


def prepared(tokens, encoder, decoders, bias):
    count = decoders.shape[0]
    rows, size = 2 * tokens[0].shape[0], encoder.shape[1]

    def kernel(mine_ref, theirs_ref, encoder_ref, decoders_ref, bias_ref, *refs):
        pre_ref, act_ref, weight_ref, sems = refs[0], refs[1], refs[2], refs[-1]
        sources = [encoder_ref] + [decoders_ref.at[k] for k in range(count)]
        copies = [
            pltpu.make_async_copy(source, refs[2 + k], sems.at[k]) for k, source in enumerate(sources)
        ]
        for copy in copies:
            copy.start()
        token = stacked([mine_ref, theirs_ref])
        copies[0].wait()
        encode(token, weight_ref, bias_ref, pre_ref, act_ref)
        for copy in copies[1:]:
            copy.wait()

    out_shape = [shape((rows, size), f32), shape((rows, size), bf16)]
    out_shape += [pltpu.VMEM(encoder.shape, encoder.dtype)]
    out_shape += [pltpu.VMEM(decoders.shape[1:], decoders.dtype)] * count
    encoder = pltpu.with_memory_space_constraint(encoder, pltpu.HBM)
    decoders = pltpu.with_memory_space_constraint(decoders, pltpu.HBM)
    in_specs = [VMEM, VMEM, HBM, HBM, VMEM]
    scratch = [pltpu.SemaphoreType.DMA((1 + count,))]
    args = [*tokens, encoder, decoders, bias]
    return call("prepared", kernel, 2 * rows * encoder.size, args, out_shape, 8, in_specs, scratch=scratch)


def chunk(tokens, encoder, bias, decoders):
    rows, size = tokens[0].shape[0], encoder.shape[1]
    width = len(decoders) * decoders[0].shape[1]

    def kernel(mine_ref, theirs_ref, encoder_ref, bias_ref, *refs):
        pre_ref, act_ref, out_ref, other_ref = refs[len(decoders) :]
        encode(stacked([mine_ref, theirs_ref]), encoder_ref, bias_ref, pre_ref, act_ref)
        decode(act_ref, refs[: len(decoders)], out_ref, other_ref)

    out_shape = [shape((2 * rows, size), f32), shape((2 * rows, size), bf16)]
    out_shape += [shape((rows, width), f32), shape((rows, width), bf16)]
    flops = 4 * rows * (encoder.size + len(decoders) * decoders[0].size)
    return call("chunk", kernel, flops, [*tokens, encoder, bias, *decoders], out_shape, 8)


def decoded(act, decoders):
    rows, width = act.shape[0] // 2, len(decoders) * decoders[0].shape[1]

    def kernel(act_ref, *refs):
        decode(act_ref, refs[: len(decoders)], *refs[len(decoders) :])

    out_shape = [shape((rows, width), f32), shape((rows, width), bf16)]
    flops = 4 * rows * len(decoders) * decoders[0].size
    return call("decoded", kernel, flops, [act, *decoders], out_shape, 8)


def transposed(weight):
    rows, columns = weight.shape
    tile = min(256, rows)

    def kernel(weight_ref, out_ref):
        @pl.loop(0, rows // tile)
        def _(i):
            at = pl.ds(pl.multiple_of(i * tile, tile), tile)
            out_ref[:, at] = weight_ref[at, :].T

    out_shape = [pltpu.VMEM((columns, rows), weight.dtype)]
    return call("transposed", kernel, 256 * rows * columns, [weight], out_shape, 4)[0]


def first_window(here, weight, entries):
    rows, width = here[0].shape
    size = weight.shape[1]

    def kernel(mine_ref, theirs_ref, weight_ref, *outs):
        first_back([mine_ref, theirs_ref], weight_ref, entries, *outs)

    out_shape = [shape((2 * rows, size), f32), shape((1, width), f32), shape((1, width), f32)]
    return call("first_window", kernel, 4 * rows * weight.size, [*here, weight], out_shape, 8)


def window(here, later, weights, back, pre, entries, acts=(), heres=()):
    rows, width = here[0].shape
    size = weights[0].shape[1]
    count = len(acts)

    def kernel(*refs):
        refs = list(refs)
        here_refs, later_refs, weight_refs = refs[:2], refs[2:4], refs[4:6]
        act_refs, heres_refs = refs[8 : 8 + count], refs[8 + count : 8 + 3 * count]
        outs = refs[8 + 3 * count :]
        second_back(later_refs, weight_refs[1], refs[6], refs[7], *outs[:2])
        first_back(here_refs, weight_refs[0], entries, *outs[2:5])
        if count:
            outers([(act_refs, heres_refs, outs[5].at[0])], *outs[6:])

    out_shape = [shape((2 * rows, size), bf16), shape((1, size), f32)]
    out_shape += [shape((2 * rows, size), f32), shape((1, width), f32), shape((1, width), f32)]
    out_specs, scratch = [VMEM] * 5, []
    flops = 8 * rows * weights[0].size
    if count:
        out_shape.append(shape((2, size, width), bf16))
        out_specs.append(ANY)
        scratch = outer_scratch(size, width)
        flops += 4 * rows * count * size * width
    args = [*here, *later, *weights, back, pre, *acts, *heres]
    limit = 10 if count else 6
    return call("window", kernel, flops, args, out_shape, limit, None, out_specs, scratch)


def tail(later, weight, back, pre, acts, laters, tokens, dpres, dec_grad):
    rows, width = later[0].shape
    size = weight.shape[1]
    count = len(acts)

    def kernel(*refs):
        refs = list(refs)
        act_refs, later_refs = refs[5 : 5 + count], refs[5 + count : 5 + 3 * count]
        token_refs, dpre_refs = refs[5 + 3 * count : 5 + 5 * count], refs[5 + 5 * count : 4 + 6 * count]
        outs = refs[5 + 6 * count :]
        sum_ref, dec_ref, enc_ref, last_ref, *buffers = outs
        second_back(refs[:2], refs[2], refs[3], refs[4], last_ref, sum_ref)
        dec_job = act_refs, later_refs, dec_ref.at[1]
        outers([dec_job, (token_refs, [*dpre_refs, last_ref], enc_ref.at[0])], *buffers)

    args = [*later, weight, back, pre, *acts, *laters, *tokens, *dpres, dec_grad]
    out_shape = [shape((1, size), f32), shape(dec_grad.shape, bf16), shape((1, width, size), bf16)]
    most = max(size, width)
    scratch = [pltpu.VMEM((2 * rows, size), bf16), *outer_scratch(most, most)]
    flops = 4 * rows * weight.size + 8 * rows * count * size * width
    in_specs = [VMEM] * (len(args) - 1) + [ANY]
    out_specs = [VMEM, ANY, ANY]
    aliases = {len(args) - 1: 1}
    return call("tail", kernel, flops, args, out_shape, 11, in_specs, out_specs, scratch, aliases)


def shards(inputs, targets, enc_weight, enc_bias, dec_weight, dec_bias):
    rows = inputs.shape[1]
    width = dec_weight.shape[3]
    layers, chips = lax.axis_size("layer"), lax.axis_size("feat") // 2
    layer = jnp.zeros((width,), f32) + lax.axis_index("layer").astype(f32)
    held, layer = lax.optimization_barrier((inputs[0], layer))
    inner, final = layer > 0.0, layer == layers - 1.0

    tokens = [(held, swapped(held))]
    pre, act, encoder, *decoders = prepared(tokens[0], enc_weight[0], dec_weight[0], enc_bias)
    pres, acts, sums = [pre], [act], [None] * chips

    def spread(j, mine, theirs):
        both = mine + swapped(theirs).astype(f32)
        later = both[:, width:].astype(bf16)
        sums[j] = both[:, :width], round_layers(later, 1)
        return later

    def run(j, *others):
        held, other = tokens[j]
        pre, act, mine, theirs = chunk((after(held, *others), other), encoder, enc_bias, decoders)
        pres.append(pre)
        acts.append(act)
        return mine, theirs

    def summed(j):
        here, later = sums[j]
        return here + jnp.where(inner, later.astype(f32), 0.0)

    order = list(range(1, chips)) + [0]
    total, done = None, acts[0]
    if chips > 1:
        held = after(from_below(tokens[0][0]), done)
        tokens.append((held, swapped(held)))
    for j in order:
        if j == 0:
            break
        mine, theirs = run(j, *([total] if j > 2 else [done]))
        if j == 1:
            first = decoded(after(acts[0], theirs), decoders)
            done = first[1]
        if j < chips - 1:
            theirs, held, done = lax.optimization_barrier((theirs, from_below(tokens[-1][0]), done))
            tokens.append((held, swapped(held)))
        if j == 2:
            total = summed(1)
        if j > 2:
            arrived = from_below(total.astype(bf16)).astype(f32)
            total = arrived + summed(j - 1)
            theirs = after(theirs, total)
        done = spread(j, mine, theirs)
        if j == 1:
            spread(0, *first)
    if chips < 3:
        total = summed(order[0])
    decoders_t = []
    for j in order[max(chips - 2, 1) :]:
        arrived = from_below(total.astype(bf16))
        if len(decoders_t) < len(decoders):
            decoders_t.append(transposed(after(decoders[len(decoders_t)], total)))
            arrived = after(arrived, decoders_t[-1])
        total = arrived.astype(f32) + summed(j)
    decoders_t += [transposed(decoder) for decoder in decoders[len(decoders_t) :]]

    grad = (total + dec_bias[0] - targets[0].astype(f32)).astype(bf16)

    entries = layers * lax.axis_size("feat") * rows * width
    here, later, dpres, sums_f, sums_d, squares = [(grad, swapped(grad))], [], [], [], [], []
    back, sum_d, square = first_window(here[0], decoders_t[0], entries)
    sums_d.append(sum_d)
    squares.append(square)
    done = back
    for j in range(chips):
        ahead = after(round_layers(here[j][0], -1), done)
        ahead = jnp.where(final, jnp.zeros_like(ahead), ahead)
        later.append((ahead, swapped(ahead)))
        if j < chips - 1:
            held = after(from_below(here[j][0]), done)
            here.append((held, swapped(held)))
            last = {}
            if j == chips - 2:
                last = {"acts": acts, "heres": [part for pair in here for part in pair]}
            dpre, sum_f, back, sum_d, square, *dec_grad = window(
                here[j + 1], later[j], decoders_t, back, pres[j], entries, **last
            )
            dpres.append(dpre)
            sums_f.append(sum_f)
            sums_d.append(sum_d)
            squares.append(square)
            done = dpre
    square = sum(squares)
    squares = [square] + [round_layers(square, k) for k in range(1, layers)]
    laters = [part for pair in later for part in pair]
    parts = [part for pair in tokens for part in pair]
    sum_f, dec_grad, enc_grad = tail(
        later[-1], decoders_t[1], back, pres[-1], acts, laters, parts, dpres, dec_grad[0]
    )
    sums_f.append(sum_f)
    squares = lax.optimization_barrier((sum_f, *squares))[1:]
    return (jnp.sum(sum(squares)), enc_grad, sum(sums_f), dec_grad[None], sum(sums_d))


def solution(mesh):
    return jax.shard_map(
        shards,
        mesh=mesh,
        in_specs=(
            P("layer", "feat", None),
            P("layer", "feat", None),
            P("layer", None, "feat"),
            P("layer", "feat"),
            P("layer", None, "feat", None),
            P("layer", None),
        ),
        out_specs=(
            P(),
            P("layer", None, "feat"),
            P("layer", "feat"),
            P("layer", None, "feat", None),
            P("layer", None),
        ),
        check_vma=False,
    )
```

```python
import math

import jax
import jax.numpy as jnp
from jax import lax
from jax.experimental import pallas as pl
from jax.experimental.pallas import tpu as pltpu
from jax.sharding import PartitionSpec as P

f32, bf16 = jnp.float32, jnp.bfloat16
MIB = 2**20
VMEM = pl.BlockSpec(memory_space=pltpu.VMEM)
HBM = pl.BlockSpec(memory_space=pltpu.HBM)
ANY = pl.BlockSpec(memory_space=pl.ANY)


def swapped(block):
    size = lax.axis_size("feat")
    return lax.ppermute(block, "feat", [(i, i ^ 1) for i in range(size)])


def from_below(block, distance=1):
    size = lax.axis_size("feat")
    return lax.ppermute(block, "feat", [(i, (i + 2 * distance) % size) for i in range(size)])


def round_layers(block, distance):
    size = lax.axis_size("layer")
    return lax.ppermute(block, "layer", [(i, (i + distance) % size) for i in range(size)])


def after(value, *others):
    return lax.optimization_barrier((value, *others))[0]


def shape(dims, dtype):
    return jax.ShapeDtypeStruct(dims, dtype)


def call(name, kernel, flops, args, out_shape, limit, in_specs=None, out_specs=None, scratch=(), aliases=None):
    size = sum(math.prod(a.shape) * jnp.dtype(a.dtype).itemsize for a in (*args, *out_shape))
    return pl.pallas_call(
        kernel,
        in_specs=in_specs or [VMEM] * len(args),
        out_specs=out_specs or [VMEM] * len(out_shape),
        out_shape=out_shape,
        scratch_shapes=scratch,
        input_output_aliases=aliases or {},
        name=name,
        compiler_params=pltpu.CompilerParams(vmem_limit_bytes=limit * MIB),
        cost_estimate=pl.CostEstimate(flops=flops, bytes_accessed=size, transcendentals=0),
    )(*args)


def stacked(refs, at=slice(None)):
    return jnp.concatenate([ref[:, at] for ref in refs], axis=0)


def column_sums(values):
    return jnp.sum(values, axis=0, keepdims=True)


def over_tiles(size, body):
    tile = min(2048, size)

    @pl.loop(0, size // tile)
    def _(i):
        body(pl.ds(pl.multiple_of(i * tile, tile), tile))


def encode(token, weight_ref, bias_ref, pre_ref, act_ref):
    def body(at):
        pre = jnp.dot(token, weight_ref[:, at], preferred_element_type=f32) + bias_ref[:, at]
        pre = jnp.maximum(pre, 0.0)
        pre_ref[:, at] = pre
        act_ref[:, at] = (pre * pre).astype(bf16)

    over_tiles(weight_ref.shape[1], body)


def decode(act_ref, weight_refs, mine_ref, theirs_ref):
    rows = mine_ref.shape[0]
    width = weight_refs[0].shape[1]
    tile = min(2048, width)
    for k, weight_ref in enumerate(weight_refs):

        @pl.loop(0, width // tile)
        def _(i, k=k, weight_ref=weight_ref):
            at = pl.ds(pl.multiple_of(i * tile, tile), tile)
            to = pl.ds(pl.multiple_of(k * width + i * tile, tile), tile)
            out = jnp.dot(act_ref[...], weight_ref[:, at], preferred_element_type=f32)
            mine_ref[:, to] = out[:rows]
            theirs_ref[:, to] = out[rows:].astype(bf16)


def first_back(grad_refs, weight_ref, back_ref, sum_ref, square_ref):
    grad = stacked(grad_refs)
    wide = grad.astype(f32)
    sum_ref[...] += column_sums(wide)
    if square_ref is not None:
        square_ref[...] = column_sums(wide * wide)

    def body(at):
        back_ref[:, at] = jnp.dot(grad, weight_ref[:, at], preferred_element_type=f32)

    over_tiles(weight_ref.shape[1], body)


def second_back(grad_refs, weight_ref, back_ref, pre_ref, dpre_ref, sum_ref):
    grad = stacked(grad_refs)

    def body(at):
        out = back_ref[:, at] + jnp.dot(grad, weight_ref[:, at], preferred_element_type=f32)
        dpre = (out * 2.0 * pre_ref[:, at]).astype(bf16)
        dpre_ref[:, at] = dpre
        sum_ref[:, at] += column_sums(dpre.astype(f32))

    over_tiles(weight_ref.shape[1], body)


def outers(jobs, buffer_ref, sem_ref):
    copies = []
    for left_refs, right_refs, out_ref in jobs:
        rows, columns = out_ref.shape
        high, wide = min(1024, rows), min(512, columns)
        for start in range(0, rows, high):
            slot = len(copies) % 2
            if len(copies) >= 2:
                copies[-2].wait()
            turned = stacked(left_refs, pl.ds(start, high)).T
            for at in range(0, columns, wide):
                at = pl.ds(at, wide)
                out = jnp.dot(turned, stacked(right_refs, at), preferred_element_type=f32)
                buffer_ref[slot, :high, at] = out.astype(bf16)
            source = buffer_ref.at[slot, :high, :columns]
            copy = pltpu.make_async_copy(source, out_ref.at[pl.ds(start, high)], sem_ref.at[slot])
            copy.start()
            copies.append(copy)
    for copy in copies[-2:]:
        copy.wait()


def outer_scratch(rows, columns):
    return [pltpu.VMEM((2, min(1024, rows), columns), bf16), pltpu.SemaphoreType.DMA((2,))]


def prepared(tokens, encoder, decoders, bias):
    count = decoders.shape[0]
    rows, size = 2 * tokens[0].shape[0], encoder.shape[1]

    def kernel(mine_ref, theirs_ref, encoder_ref, decoders_ref, bias_ref, *refs):
        pre_ref, act_ref, weight_ref = refs[:3]
        mine, bias, sems = refs[-3:]
        sources = [mine_ref, bias_ref, encoder_ref] + [decoders_ref.at[k] for k in range(count)]
        targets = [mine, bias, *refs[2 : 3 + count]]
        copies = [
            pltpu.make_async_copy(source, target, sems.at[k])
            for k, (source, target) in enumerate(zip(sources, targets))
        ]
        for copy in copies:
            copy.start()
        for copy in copies[:3]:
            copy.wait()
        encode(stacked([mine, theirs_ref]), weight_ref, bias, pre_ref, act_ref)
        for copy in copies[3:]:
            copy.wait()

    out_shape = [shape((rows, size), f32), shape((rows, size), bf16)]
    out_shape += [pltpu.VMEM(encoder.shape, encoder.dtype)]
    out_shape += [pltpu.VMEM(decoders.shape[1:], decoders.dtype)] * count
    scratch = [pltpu.VMEM(tokens[0].shape, bf16), pltpu.VMEM(bias.shape, f32)]
    scratch.append(pltpu.SemaphoreType.DMA((3 + count,)))
    args = [tokens[0], encoder, decoders, bias]
    args = [pltpu.with_memory_space_constraint(array, pltpu.HBM) for array in args]
    args.insert(1, tokens[1])
    in_specs = [HBM, VMEM, HBM, HBM, HBM]
    return call("prepared", kernel, 2 * rows * encoder.size, args, out_shape, 8, in_specs, scratch=scratch)


def chunk(tokens, encoder, bias, decoders):
    rows, size = tokens[0].shape[0], encoder.shape[1]
    width = len(decoders) * decoders[0].shape[1]

    def kernel(mine_ref, theirs_ref, encoder_ref, bias_ref, *refs):
        pre_ref, act_ref, out_ref, other_ref = refs[len(decoders) :]
        encode(stacked([mine_ref, theirs_ref]), encoder_ref, bias_ref, pre_ref, act_ref)
        decode(act_ref, refs[: len(decoders)], out_ref, other_ref)

    out_shape = [shape((2 * rows, size), f32), shape((2 * rows, size), bf16)]
    out_shape += [shape((rows, width), f32), shape((rows, width), bf16)]
    flops = 4 * rows * (encoder.size + len(decoders) * decoders[0].size)
    return call("chunk", kernel, flops, [*tokens, encoder, bias, *decoders], out_shape, 8)


def decoded(act, decoders):
    rows, width = act.shape[0] // 2, len(decoders) * decoders[0].shape[1]

    def kernel(act_ref, *refs):
        decode(act_ref, refs[: len(decoders)], *refs[len(decoders) :])

    out_shape = [shape((rows, width), f32), shape((rows, width), bf16)]
    flops = 4 * rows * len(decoders) * decoders[0].size
    return call("decoded", kernel, flops, [act, *decoders], out_shape, 8)


def transposed(weight):
    rows, columns = weight.shape
    tile = min(256, rows)

    def kernel(weight_ref, out_ref):
        @pl.loop(0, rows // tile)
        def _(i):
            at = pl.ds(pl.multiple_of(i * tile, tile), tile)
            out_ref[:, at] = weight_ref[at, :].T

    out_shape = [pltpu.VMEM((columns, rows), weight.dtype)]
    return call("transposed", kernel, 256 * rows * columns, [weight], out_shape, 4)[0]


def backward(weights, firsts, seconds, sums, jobs=(), held=None):
    width, size = weights[0].shape
    args, places = [], {}

    def add(array):
        if id(array) not in places:
            places[id(array)] = len(args)
            args.append(array)
        return places[id(array)]

    def add_all(arrays):
        return [array if isinstance(array, int) else (add(array),) for array in arrays]

    weight_at = [add(weight) for weight in weights]
    first_at = [add_all(pair) for pair in firsts]
    second_at = [(add_all(pair), add(back), add(pre)) for pair, back, pre in seconds]
    job_at = [(add_all(left), add_all(right)) for left, right, _, _ in jobs]
    sums_at = [add(array) for array in sums]
    count, backs, dpres = len(args) + (held is not None), len(firsts), len(seconds)

    def kernel(*refs):
        ins, outs = refs[:count], refs[count:]
        dpre_refs = outs[backs : backs + dpres]
        grad_sum_ref, dpre_sum_ref = outs[backs + dpres : backs + dpres + 2]
        job_refs, scratch = outs[backs + dpres + 2 :][: len(jobs)], outs[backs + dpres + 2 + len(jobs) :]

        def pick(ats):
            return [dpre_refs[at] if isinstance(at, int) else ins[at[0]] for at in ats]

        for k, sum_ref in enumerate((grad_sum_ref, dpre_sum_ref)):
            sum_ref[...] = ins[sums_at[k]][...] if sums else jnp.zeros(sum_ref.shape, f32)
        square_ref = None if sums else outs[backs + dpres + 2]
        for at, back_ref in zip(first_at, outs):
            first_back(pick(at), ins[weight_at[0]], back_ref, grad_sum_ref, square_ref)
        for (at, back, pre), dpre_ref in zip(second_at, dpre_refs):
            second_back(pick(at), ins[weight_at[1]], ins[back], ins[pre], dpre_ref, dpre_sum_ref)
        work = [
            (pick(left), pick(right), out_ref.at[index])
            for (left, right), out_ref, (_, _, _, index) in zip(job_at, job_refs, jobs)
        ]
        if work:
            outers(work, *scratch)

    out_shape = [shape((2 * pair[0].shape[0], size), f32) for pair in firsts]
    out_shape += [shape(pre.shape, bf16) for _, _, pre in seconds]
    out_shape += [shape((1, width), f32), shape((1, size), f32)] + [shape((1, width), f32)] * (not sums)
    in_specs, out_specs = [VMEM] * len(args), [VMEM] * len(out_shape)
    flops = 2 * sum(part.size for part in out_shape[: backs + dpres]) * width
    scratch, aliases = [], {}
    for left, right, lead, _ in jobs:
        columns = size if isinstance(right[-1], int) else right[0].shape[1]
        out_shape.append(shape((lead, left[0].shape[1], columns), bf16))
        out_specs.append(ANY)
        flops += 2 * out_shape[-1].size // lead * sum(part.shape[0] for part in left)
    if jobs:
        scratch = outer_scratch(max(size, width), max(part.shape[2] for part in out_shape[-len(jobs) :]))
    if held is not None:
        aliases = {len(args): backs + dpres + 2}
        args.append(held)
        in_specs.append(ANY)
    limit = 16 if jobs else 6
    outs = call("backward", kernel, flops, args, out_shape, limit, in_specs, out_specs, scratch, aliases)
    return outs[:backs], outs[backs : backs + dpres], outs[backs + dpres :]


def shards(inputs, targets, enc_weight, enc_bias, dec_weight, dec_bias):
    rows = inputs.shape[1]
    width = dec_weight.shape[3]
    layers, chips = lax.axis_size("layer"), lax.axis_size("feat") // 2
    layer = jnp.zeros((width,), f32) + lax.axis_index("layer").astype(f32)
    held, layer = lax.optimization_barrier((inputs[0], layer))
    inner, final = layer > 0.0, layer == layers - 1.0

    tokens = [(held, swapped(held))]
    pre, act, encoder, *decoders = prepared(tokens[0], enc_weight[0], dec_weight[0], enc_bias)
    pres, acts, sums = [pre], [act], [None] * chips

    def spread(j, mine, theirs):
        both = mine + swapped(theirs).astype(f32)
        later = both[:, width:].astype(bf16)
        sums[j] = both[:, :width], round_layers(later, 1)
        return later

    def run(j, *others):
        held, other = tokens[j]
        pre, act, mine, theirs = chunk((after(held, *others), other), encoder, enc_bias, decoders)
        pres.append(pre)
        acts.append(act)
        return mine, theirs

    def summed(j):
        here, later = sums[j]
        return here + jnp.where(inner, later.astype(f32), 0.0)

    order = list(range(1, chips)) + [0]
    total, done = None, acts[0]
    if chips > 1:
        held = after(from_below(tokens[0][0]), done)
        tokens.append((held, swapped(held)))
    for j in order:
        if j == 0:
            break
        mine, theirs = run(j, *([total] if j > 2 else [done]))
        if j == 1:
            first = decoded(after(acts[0], theirs), decoders)
            done = first[1]
        if j < chips - 1:
            theirs, held, done = lax.optimization_barrier((theirs, from_below(tokens[-1][0]), done))
            tokens.append((held, swapped(held)))
        if j == 2:
            total = summed(1)
        if j > 2:
            arrived = from_below(total.astype(bf16)).astype(f32)
            total = arrived + summed(j - 1)
            theirs = after(theirs, total)
        done = spread(j, mine, theirs)
        if j == 1:
            spread(0, *first)
    if chips < 3:
        total = summed(order[0])
    decoders_t = []
    for j in order[max(chips - 2, 1) :]:
        arrived = from_below(total.astype(bf16))
        if len(decoders_t) < len(decoders):
            decoders_t.append(transposed(after(decoders[len(decoders_t)], total)))
            arrived = after(arrived, decoders_t[-1])
        total = arrived.astype(f32) + summed(j)
    decoders_t += [transposed(decoder) for decoder in decoders[len(decoders_t) :]]

    grad = (total + dec_bias[0] - targets[0].astype(f32)).astype(bf16)

    here, later, backs, dpres, acc = [(grad, swapped(grad))], [], [], [], []
    (back,), _, (*acc, squares) = backward(decoders_t, here, [], [])
    done, dec_grad, pending = back, None, []
    entries = layers * lax.axis_size("feat") * rows * width
    hops = [[(from_below, k) for k in range(1, chips)], [(round_layers, k) for k in range(1, layers)]]
    for j in range(chips):
        if j < chips - 1:
            held = done = after(from_below(here[j][0]), done)
        ahead = after(round_layers(here[j][0], -1), done)
        ahead = jnp.where(final, jnp.zeros_like(ahead), ahead)
        if pending:
            squares = sum(after(block, ahead) for block in pending) + squares
            held, ahead = lax.optimization_barrier((held, ahead, squares))[:2]
        if j < chips - 1:
            here.append((held, swapped(held)))
        later.append((ahead, swapped(ahead)))
        pending = []
        if hops and j < chips - 1:
            pending = [move(squares, distance) for move, distance in hops.pop(0)]
        if j == chips - 1:
            break
        jobs = []
        if j == chips - 2:
            jobs = [(acts, [part for pair in here for part in pair], 2, 0)]
        (back,), (dpre,), acc = backward(
            decoders_t, [here[j + 1]], [(later[j], back, pres[j])], acc[:2], jobs
        )
        dpres.append(dpre)
        done, dec_grad = dpre, acc[-1]

    flat = [part for pair in tokens for part in pair]
    jobs = [(acts, [part for pair in later for part in pair], 2, 1), (flat, [*dpres, 0], 1, 0)]
    _, _, (grad_sum, dpre_sum, dec_grad, enc_grad) = backward(
        decoders_t, [], [(later[-1], back, pres[-1])], acc[:2], jobs, dec_grad
    )
    for moves in hops:
        squares = sum(move(squares, distance) for move, distance in moves) + squares
    return (jnp.sum(squares / entries), enc_grad, dpre_sum, dec_grad[None], grad_sum)


def solution(mesh):
    return jax.shard_map(
        shards,
        mesh=mesh,
        in_specs=(
            P("layer", "feat", None),
            P("layer", "feat", None),
            P("layer", None, "feat"),
            P("layer", "feat"),
            P("layer", None, "feat", None),
            P("layer", None),
        ),
        out_specs=(
            P(),
            P("layer", None, "feat"),
            P("layer", "feat"),
            P("layer", None, "feat", None),
            P("layer", None),
        ),
        check_vma=False,
    )
```

```python
import math

import jax
import jax.numpy as jnp
from jax import lax
from jax.experimental import pallas as pl
from jax.experimental.pallas import tpu as pltpu
from jax.sharding import PartitionSpec as P

f32, bf16 = jnp.float32, jnp.bfloat16
MIB = 2**20
VMEM = pl.BlockSpec(memory_space=pltpu.VMEM)
HBM = pl.BlockSpec(memory_space=pltpu.HBM)
ANY = pl.BlockSpec(memory_space=pl.ANY)


def swapped(block):
    size = lax.axis_size("feat")
    return lax.ppermute(block, "feat", [(i, i ^ 1) for i in range(size)])


def from_below(block, distance=1):
    size = lax.axis_size("feat")
    return lax.ppermute(block, "feat", [(i, (i + 2 * distance) % size) for i in range(size)])


def round_layers(block, distance):
    size = lax.axis_size("layer")
    return lax.ppermute(block, "layer", [(i, (i + distance) % size) for i in range(size)])


def after(value, *others):
    return lax.optimization_barrier((value, *others))[0]


def shape(dims, dtype):
    return jax.ShapeDtypeStruct(dims, dtype)


def call(name, kernel, flops, args, out_shape, limit, in_specs=None, out_specs=None, scratch=(), aliases=None):
    size = sum(math.prod(a.shape) * jnp.dtype(a.dtype).itemsize for a in (*args, *out_shape))
    return pl.pallas_call(
        kernel,
        in_specs=in_specs or [VMEM] * len(args),
        out_specs=out_specs or [VMEM] * len(out_shape),
        out_shape=out_shape,
        scratch_shapes=scratch,
        input_output_aliases=aliases or {},
        name=name,
        compiler_params=pltpu.CompilerParams(vmem_limit_bytes=limit * MIB),
        cost_estimate=pl.CostEstimate(flops=flops, bytes_accessed=size, transcendentals=0),
    )(*args)


def stacked(refs, at=slice(None)):
    return jnp.concatenate([ref[:, at] for ref in refs], axis=0)


def column_sums(values):
    return jnp.sum(values, axis=0, keepdims=True)


def over_tiles(size, body):
    tile = min(1024, size)

    @pl.loop(0, size // tile)
    def _(i):
        body(pl.ds(pl.multiple_of(i * tile, tile), tile))


def encode(token, weight_ref, bias_ref, pre_ref, act_ref):
    def body(at):
        pre = jnp.dot(token, weight_ref[:, at], preferred_element_type=f32) + bias_ref[:, at]
        pre = jnp.maximum(pre, 0.0)
        pre_ref[:, at] = pre
        act_ref[:, at] = (pre * pre).astype(bf16)

    over_tiles(weight_ref.shape[1], body)


def decode(act_ref, weight_refs, mine_ref, theirs_ref):
    rows = mine_ref.shape[0]
    width = weight_refs[0].shape[1]
    tile = min(1024, width)
    for k, weight_ref in enumerate(weight_refs):

        @pl.loop(0, width // tile)
        def _(i, k=k, weight_ref=weight_ref):
            at = pl.ds(pl.multiple_of(i * tile, tile), tile)
            to = pl.ds(pl.multiple_of(k * width + i * tile, tile), tile)
            out = jnp.dot(act_ref[...], weight_ref[:, at], preferred_element_type=f32)
            mine_ref[:, to] = out[:rows]
            theirs_ref[:, to] = out[rows:].astype(bf16)


def first_back(grad_refs, weight_ref, back_ref, sum_ref, square_ref):
    grad = stacked(grad_refs)
    wide = grad.astype(f32)
    sum_ref[...] += column_sums(wide)
    if square_ref is not None:
        square_ref[...] = column_sums(wide * wide)

    def body(at):
        back_ref[:, at] = jnp.dot(grad, weight_ref[:, at], preferred_element_type=f32)

    over_tiles(weight_ref.shape[1], body)


def second_back(grad_refs, weight_ref, back_ref, pre_ref, dpre_ref, sum_ref):
    grad = stacked(grad_refs)

    def body(at):
        out = back_ref[:, at] + jnp.dot(grad, weight_ref[:, at], preferred_element_type=f32)
        dpre = (out * 2.0 * pre_ref[:, at]).astype(bf16)
        dpre_ref[:, at] = dpre
        sum_ref[:, at] += column_sums(dpre.astype(f32))

    over_tiles(weight_ref.shape[1], body)


def outers(jobs, buffer_ref, sem_ref):
    copies = []
    for left_refs, right_refs, out_ref in jobs:
        rows, columns = out_ref.shape
        high, wide = min(1024, rows), min(512, columns)
        for start in range(0, rows, high):
            slot = len(copies) % 2
            if len(copies) >= 2:
                copies[-2].wait()
            turned = stacked(left_refs, pl.ds(start, high)).T
            for at in range(0, columns, wide):
                at = pl.ds(at, wide)
                out = jnp.dot(turned, stacked(right_refs, at), preferred_element_type=f32)
                buffer_ref[slot, :high, at] = out.astype(bf16)
            source = buffer_ref.at[slot, :high, :columns]
            copy = pltpu.make_async_copy(source, out_ref.at[pl.ds(start, high)], sem_ref.at[slot])
            copy.start()
            copies.append(copy)
    for copy in copies[-2:]:
        copy.wait()


def outer_scratch(rows, columns):
    return [pltpu.VMEM((2, min(1024, rows), columns), bf16), pltpu.SemaphoreType.DMA((2,))]


def prepared(tokens, encoder, decoders, bias):
    count = decoders.shape[0]
    rows, size = 2 * tokens[0].shape[0], encoder.shape[1]

    def kernel(mine_ref, theirs_ref, encoder_ref, decoders_ref, bias_ref, *refs):
        pre_ref, act_ref, weight_ref = refs[:3]
        mine, bias, sems = refs[-3:]
        sources = [mine_ref, bias_ref, encoder_ref] + [decoders_ref.at[k] for k in range(count)]
        targets = [mine, bias, *refs[2 : 3 + count]]
        copies = [
            pltpu.make_async_copy(source, target, sems.at[k])
            for k, (source, target) in enumerate(zip(sources, targets))
        ]
        for copy in copies:
            copy.start()
        for copy in copies[:3]:
            copy.wait()
        encode(stacked([mine, theirs_ref]), weight_ref, bias, pre_ref, act_ref)
        for copy in copies[3:]:
            copy.wait()

    out_shape = [shape((rows, size), f32), shape((rows, size), bf16)]
    out_shape += [pltpu.VMEM(encoder.shape, encoder.dtype)]
    out_shape += [pltpu.VMEM(decoders.shape[1:], decoders.dtype)] * count
    scratch = [pltpu.VMEM(tokens[0].shape, bf16), pltpu.VMEM(bias.shape, f32)]
    scratch.append(pltpu.SemaphoreType.DMA((3 + count,)))
    args = [tokens[0], encoder, decoders, bias]
    args = [pltpu.with_memory_space_constraint(array, pltpu.HBM) for array in args]
    args.insert(1, tokens[1])
    in_specs = [HBM, VMEM, HBM, HBM, HBM]
    return call("prepared", kernel, 2 * rows * encoder.size, args, out_shape, 8, in_specs, scratch=scratch)


def chunk(tokens, encoder, bias, decoders):
    rows, size = tokens[0].shape[0], encoder.shape[1]
    width = len(decoders) * decoders[0].shape[1]

    def kernel(mine_ref, theirs_ref, encoder_ref, bias_ref, *refs):
        pre_ref, act_ref, out_ref, other_ref = refs[len(decoders) :]
        encode(stacked([mine_ref, theirs_ref]), encoder_ref, bias_ref, pre_ref, act_ref)
        decode(act_ref, refs[: len(decoders)], out_ref, other_ref)

    out_shape = [shape((2 * rows, size), f32), shape((2 * rows, size), bf16)]
    out_shape += [shape((rows, width), f32), shape((rows, width), bf16)]
    flops = 4 * rows * (encoder.size + len(decoders) * decoders[0].size)
    return call("chunk", kernel, flops, [*tokens, encoder, bias, *decoders], out_shape, 8)


def decoded(act, decoders):
    rows, width = act.shape[0] // 2, len(decoders) * decoders[0].shape[1]

    def kernel(act_ref, *refs):
        decode(act_ref, refs[: len(decoders)], *refs[len(decoders) :])

    out_shape = [shape((rows, width), f32), shape((rows, width), bf16)]
    flops = 4 * rows * len(decoders) * decoders[0].size
    return call("decoded", kernel, flops, [act, *decoders], out_shape, 8)


def transposed(weight):
    rows, columns = weight.shape
    tile = min(256, rows)

    def kernel(weight_ref, out_ref):
        @pl.loop(0, rows // tile)
        def _(i):
            at = pl.ds(pl.multiple_of(i * tile, tile), tile)
            out_ref[:, at] = weight_ref[at, :].T

    out_shape = [pltpu.VMEM((columns, rows), weight.dtype)]
    return call("transposed", kernel, 256 * rows * columns, [weight], out_shape, 4)[0]


def backward(weights, firsts, seconds, sums, jobs=(), held=None):
    width, size = weights[0].shape
    args, places = [], {}

    def add(array):
        if id(array) not in places:
            places[id(array)] = len(args)
            args.append(array)
        return places[id(array)]

    def add_all(arrays):
        return [array if isinstance(array, int) else (add(array),) for array in arrays]

    weight_at = [add(weight) for weight in weights]
    first_at = [add_all(pair) for pair in firsts]
    second_at = [(add_all(pair), add(back), add(pre)) for pair, back, pre in seconds]
    job_at = [(add_all(left), add_all(right)) for left, right, _, _ in jobs]
    sums_at = [add(array) for array in sums]
    count, backs, dpres = len(args) + (held is not None), len(firsts), len(seconds)

    def kernel(*refs):
        ins, outs = refs[:count], refs[count:]
        dpre_refs = outs[backs : backs + dpres]
        grad_sum_ref, dpre_sum_ref = outs[backs + dpres : backs + dpres + 2]
        job_refs, scratch = outs[backs + dpres + 2 :][: len(jobs)], outs[backs + dpres + 2 + len(jobs) :]

        def pick(ats):
            return [dpre_refs[at] if isinstance(at, int) else ins[at[0]] for at in ats]

        for k, sum_ref in enumerate((grad_sum_ref, dpre_sum_ref)):
            sum_ref[...] = ins[sums_at[k]][...] if sums else jnp.zeros(sum_ref.shape, f32)
        square_ref = None if sums else outs[backs + dpres + 2]
        for at, back_ref in zip(first_at, outs):
            first_back(pick(at), ins[weight_at[0]], back_ref, grad_sum_ref, square_ref)
        for (at, back, pre), dpre_ref in zip(second_at, dpre_refs):
            second_back(pick(at), ins[weight_at[1]], ins[back], ins[pre], dpre_ref, dpre_sum_ref)
        work = [
            (pick(left), pick(right), out_ref.at[index])
            for (left, right), out_ref, (_, _, _, index) in zip(job_at, job_refs, jobs)
        ]
        if work:
            outers(work, *scratch)

    out_shape = [shape((2 * pair[0].shape[0], size), f32) for pair in firsts]
    out_shape += [shape(pre.shape, bf16) for _, _, pre in seconds]
    out_shape += [shape((1, width), f32), shape((1, size), f32)] + [shape((1, width), f32)] * (not sums)
    in_specs, out_specs = [VMEM] * len(args), [VMEM] * len(out_shape)
    flops = 2 * sum(part.size for part in out_shape[: backs + dpres]) * width
    scratch, aliases = [], {}
    for left, right, lead, _ in jobs:
        columns = size if isinstance(right[-1], int) else right[0].shape[1]
        out_shape.append(shape((lead, left[0].shape[1], columns), bf16))
        out_specs.append(ANY)
        flops += 2 * out_shape[-1].size // lead * sum(part.shape[0] for part in left)
    if jobs:
        scratch = outer_scratch(max(size, width), max(part.shape[2] for part in out_shape[-len(jobs) :]))
    if held is not None:
        aliases = {len(args): backs + dpres + 2}
        args.append(held)
        in_specs.append(ANY)
    limit = 16 if jobs else 6
    outs = call("backward", kernel, flops, args, out_shape, limit, in_specs, out_specs, scratch, aliases)
    return outs[:backs], outs[backs : backs + dpres], outs[backs + dpres :]


def shards(inputs, targets, enc_weight, enc_bias, dec_weight, dec_bias):
    rows = inputs.shape[1]
    width = dec_weight.shape[3]
    layers, chips = lax.axis_size("layer"), lax.axis_size("feat") // 2
    layer = jnp.zeros((width,), f32) + lax.axis_index("layer").astype(f32)
    held, layer = lax.optimization_barrier((inputs[0], layer))
    inner, final = layer > 0.0, layer == layers - 1.0

    tokens = [(held, swapped(held))]
    pre, act, encoder, *decoders = prepared(tokens[0], enc_weight[0], dec_weight[0], enc_bias)
    pres, acts, sums = [pre], [act], [None] * chips

    def spread(j, mine, theirs):
        both = mine + swapped(theirs).astype(f32)
        later = both[:, width:].astype(bf16)
        sums[j] = both[:, :width], round_layers(later, 1)
        return later

    def run(j, *others):
        held, other = tokens[j]
        pre, act, mine, theirs = chunk((after(held, *others), other), encoder, enc_bias, decoders)
        pres.append(pre)
        acts.append(act)
        return mine, theirs

    def summed(j):
        here, later = sums[j]
        return here + jnp.where(inner, later.astype(f32), 0.0)

    order = list(range(1, chips)) + [0]
    total, done = None, acts[0]
    if chips > 1:
        held = after(from_below(tokens[0][0]), done)
        tokens.append((held, swapped(held)))
    for j in order:
        if j == 0:
            break
        mine, theirs = run(j, *([total] if j > 2 else [done]))
        if j == 1:
            first = decoded(after(acts[0], theirs), decoders)
            done = first[1]
        if j < chips - 1:
            theirs, held, done = lax.optimization_barrier((theirs, from_below(tokens[-1][0]), done))
            tokens.append((held, swapped(held)))
        if j == 2:
            total = summed(1)
        if j > 2:
            arrived = from_below(total.astype(bf16)).astype(f32)
            total = arrived + summed(j - 1)
            theirs = after(theirs, total)
        done = spread(j, mine, theirs)
        if j == 1:
            spread(0, *first)
    if chips < 3:
        total = summed(order[0])
    decoders_t = []
    for j in order[max(chips - 2, 1) :]:
        arrived = from_below(total.astype(bf16))
        if len(decoders_t) < len(decoders):
            decoders_t.append(transposed(after(decoders[len(decoders_t)], total)))
            arrived = after(arrived, decoders_t[-1])
        total = arrived.astype(f32) + summed(j)
    decoders_t += [transposed(decoder) for decoder in decoders[len(decoders_t) :]]

    grad = (total + dec_bias[0] - targets[0].astype(f32)).astype(bf16)

    here, later, backs, dpres, acc = [(grad, swapped(grad))], [], [], [], []
    (back,), _, (*acc, squares) = backward(decoders_t, here, [], [])
    done, dec_grad, pending = back, None, []
    entries = layers * lax.axis_size("feat") * rows * width
    hops = [[(from_below, k) for k in range(1, chips)], [(round_layers, k) for k in range(1, layers)]]
    for j in range(chips):
        if j < chips - 1:
            held = done = after(from_below(here[j][0]), done)
        ahead = after(round_layers(here[j][0], -1), done)
        ahead = jnp.where(final, jnp.zeros_like(ahead), ahead)
        if pending:
            squares = sum(after(block, ahead) for block in pending) + squares
            held, ahead = lax.optimization_barrier((held, ahead, squares))[:2]
        if j < chips - 1:
            here.append((held, swapped(held)))
        later.append((ahead, swapped(ahead)))
        pending = []
        if hops and j < chips - 1:
            pending = [move(squares, distance) for move, distance in hops.pop(0)]
        if j == chips - 1:
            break
        jobs = []
        if j == chips - 2:
            jobs = [(acts, [part for pair in here for part in pair], 2, 0)]
        (back,), (dpre,), acc = backward(
            decoders_t, [here[j + 1]], [(later[j], back, pres[j])], acc[:2], jobs
        )
        dpres.append(dpre)
        done, dec_grad = dpre, acc[-1]

    flat = [part for pair in tokens for part in pair]
    jobs = [(acts, [part for pair in later for part in pair], 2, 1), (flat, [*dpres, 0], 1, 0)]
    _, _, (grad_sum, dpre_sum, dec_grad, enc_grad) = backward(
        decoders_t, [], [(later[-1], back, pres[-1])], acc[:2], jobs, dec_grad
    )
    for moves in hops:
        squares = sum(move(squares, distance) for move, distance in moves) + squares
    return (jnp.sum(squares / entries), enc_grad, dpre_sum, dec_grad[None], grad_sum)


def solution(mesh):
    return jax.shard_map(
        shards,
        mesh=mesh,
        in_specs=(
            P("layer", "feat", None),
            P("layer", "feat", None),
            P("layer", None, "feat"),
            P("layer", "feat"),
            P("layer", None, "feat", None),
            P("layer", None),
        ),
        out_specs=(
            P(),
            P("layer", None, "feat"),
            P("layer", "feat"),
            P("layer", None, "feat", None),
            P("layer", None),
        ),
        check_vma=False,
    )
```

```python
import math

import jax
import jax.numpy as jnp
from jax import lax
from jax.experimental import pallas as pl
from jax.experimental.pallas import tpu as pltpu
from jax.sharding import PartitionSpec as P

f32, bf16 = jnp.float32, jnp.bfloat16
MIB = 2**20
VMEM = pl.BlockSpec(memory_space=pltpu.VMEM)
HBM = pl.BlockSpec(memory_space=pltpu.HBM)
ANY = pl.BlockSpec(memory_space=pl.ANY)


def swapped(block):
    size = lax.axis_size("feat")
    return lax.ppermute(block, "feat", [(i, i ^ 1) for i in range(size)])


def from_below(block, distance=1):
    size = lax.axis_size("feat")
    return lax.ppermute(block, "feat", [(i, (i + 2 * distance) % size) for i in range(size)])


def round_layers(block, distance):
    size = lax.axis_size("layer")
    return lax.ppermute(block, "layer", [(i, (i + distance) % size) for i in range(size)])


def after(value, *others):
    return lax.optimization_barrier((value, *others))[0]


def shape(dims, dtype):
    return jax.ShapeDtypeStruct(dims, dtype)


def call(name, kernel, flops, args, out_shape, limit, in_specs=None, out_specs=None, scratch=(), aliases=None):
    size = sum(math.prod(a.shape) * jnp.dtype(a.dtype).itemsize for a in (*args, *out_shape))
    return pl.pallas_call(
        kernel,
        in_specs=in_specs or [VMEM] * len(args),
        out_specs=out_specs or [VMEM] * len(out_shape),
        out_shape=out_shape,
        scratch_shapes=scratch,
        input_output_aliases=aliases or {},
        name=name,
        compiler_params=pltpu.CompilerParams(vmem_limit_bytes=limit * MIB),
        cost_estimate=pl.CostEstimate(flops=flops, bytes_accessed=size, transcendentals=0),
    )(*args)


def stacked(refs, at=slice(None)):
    return jnp.concatenate([ref[:, at] for ref in refs], axis=0)


def column_sums(values):
    return jnp.sum(values, axis=0, keepdims=True)


def over_tiles(size, body):
    tile = min(1024, size)

    @pl.loop(0, size // tile)
    def _(i):
        body(pl.ds(pl.multiple_of(i * tile, tile), tile))


def encode(token, weight_ref, bias_ref, pre_ref, act_ref):
    def body(at):
        pre = jnp.dot(token, weight_ref[:, at], preferred_element_type=f32) + bias_ref[:, at]
        pre = jnp.maximum(pre, 0.0)
        pre_ref[:, at] = pre
        act_ref[:, at] = (pre * pre).astype(bf16)

    over_tiles(weight_ref.shape[1], body)


def decode(act_ref, weight_refs, mine_ref, theirs_ref):
    rows = mine_ref.shape[0]
    width = weight_refs[0].shape[1]
    tile = min(1024, width)
    for k, weight_ref in enumerate(weight_refs):

        @pl.loop(0, width // tile)
        def _(i, k=k, weight_ref=weight_ref):
            at = pl.ds(pl.multiple_of(i * tile, tile), tile)
            to = pl.ds(pl.multiple_of(k * width + i * tile, tile), tile)
            out = jnp.dot(act_ref[...], weight_ref[:, at], preferred_element_type=f32)
            mine_ref[:, to] = out[:rows]
            theirs_ref[:, to] = out[rows:].astype(bf16)


def first_back(grad_refs, weight_ref, back_ref, sum_ref, square_ref):
    grad = stacked(grad_refs)
    wide = grad.astype(f32)
    sum_ref[...] += column_sums(wide)
    if square_ref is not None:
        square_ref[...] = column_sums(wide * wide)

    def body(at):
        back_ref[:, at] = jnp.dot(grad, weight_ref[:, at], preferred_element_type=f32)

    over_tiles(weight_ref.shape[1], body)


def second_back(grad_refs, weight_ref, back_ref, pre_ref, dpre_ref, sum_ref):
    grad = stacked(grad_refs)

    def body(at):
        out = back_ref[:, at] + jnp.dot(grad, weight_ref[:, at], preferred_element_type=f32)
        dpre = (out * 2.0 * pre_ref[:, at]).astype(bf16)
        dpre_ref[:, at] = dpre
        sum_ref[:, at] += column_sums(dpre.astype(f32))

    over_tiles(weight_ref.shape[1], body)


def outers(jobs, buffer_ref, sem_ref):
    copies = []
    for left_refs, right_refs, out_ref in jobs:
        rows, columns = out_ref.shape
        high, wide = min(1024, rows), min(512, columns)
        for start in range(0, rows, high):
            slot = len(copies) % 2
            if len(copies) >= 2:
                copies[-2].wait()
            turned = stacked(left_refs, pl.ds(start, high)).T
            for at in range(0, columns, wide):
                at = pl.ds(at, wide)
                out = jnp.dot(turned, stacked(right_refs, at), preferred_element_type=f32)
                buffer_ref[slot, :high, at] = out.astype(bf16)
            source = buffer_ref.at[slot, :high, :columns]
            copy = pltpu.make_async_copy(source, out_ref.at[pl.ds(start, high)], sem_ref.at[slot])
            copy.start()
            copies.append(copy)
    for copy in copies[-2:]:
        copy.wait()


def outer_scratch(rows, columns):
    return [pltpu.VMEM((2, min(1024, rows), columns), bf16), pltpu.SemaphoreType.DMA((2,))]


def prepared(tokens, encoder, decoders, bias):
    count = decoders.shape[0]
    rows, size = 2 * tokens[0].shape[0], encoder.shape[1]

    def kernel(mine_ref, theirs_ref, encoder_ref, decoders_ref, bias_ref, *refs):
        pre_ref, act_ref, weight_ref = refs[:3]
        mine, bias, sems = refs[-3:]
        sources = [mine_ref, bias_ref, encoder_ref] + [decoders_ref.at[k] for k in range(count)]
        targets = [mine, bias, *refs[2 : 3 + count]]
        copies = [
            pltpu.make_async_copy(source, target, sems.at[k])
            for k, (source, target) in enumerate(zip(sources, targets))
        ]
        for copy in copies:
            copy.start()
        for copy in copies[:3]:
            copy.wait()
        encode(stacked([mine, theirs_ref]), weight_ref, bias, pre_ref, act_ref)
        for copy in copies[3:]:
            copy.wait()

    out_shape = [shape((rows, size), f32), shape((rows, size), bf16)]
    out_shape += [pltpu.VMEM(encoder.shape, encoder.dtype)]
    out_shape += [pltpu.VMEM(decoders.shape[1:], decoders.dtype)] * count
    scratch = [pltpu.VMEM(tokens[0].shape, bf16), pltpu.VMEM(bias.shape, f32)]
    scratch.append(pltpu.SemaphoreType.DMA((3 + count,)))
    args = [tokens[0], encoder, decoders, bias]
    args = [pltpu.with_memory_space_constraint(array, pltpu.HBM) for array in args]
    args.insert(1, tokens[1])
    in_specs = [HBM, VMEM, HBM, HBM, HBM]
    return call("prepared", kernel, 2 * rows * encoder.size, args, out_shape, 8, in_specs, scratch=scratch)


def chunk(tokens, encoder, bias, decoders):
    rows, size = tokens[0].shape[0], encoder.shape[1]
    width = len(decoders) * decoders[0].shape[1]

    def kernel(mine_ref, theirs_ref, encoder_ref, bias_ref, *refs):
        pre_ref, act_ref, out_ref, other_ref = refs[len(decoders) :]
        encode(stacked([mine_ref, theirs_ref]), encoder_ref, bias_ref, pre_ref, act_ref)
        decode(act_ref, refs[: len(decoders)], out_ref, other_ref)

    out_shape = [shape((2 * rows, size), f32), shape((2 * rows, size), bf16)]
    out_shape += [shape((rows, width), f32), shape((rows, width), bf16)]
    flops = 4 * rows * (encoder.size + len(decoders) * decoders[0].size)
    return call("chunk", kernel, flops, [*tokens, encoder, bias, *decoders], out_shape, 8)


def decoded(act, decoders):
    rows, width = act.shape[0] // 2, len(decoders) * decoders[0].shape[1]

    def kernel(act_ref, *refs):
        decode(act_ref, refs[: len(decoders)], *refs[len(decoders) :])

    out_shape = [shape((rows, width), f32), shape((rows, width), bf16)]
    flops = 4 * rows * len(decoders) * decoders[0].size
    return call("decoded", kernel, flops, [act, *decoders], out_shape, 8)


def transposed(weight):
    rows, columns = weight.shape
    tile = min(256, rows)

    def kernel(weight_ref, out_ref):
        @pl.loop(0, rows // tile)
        def _(i):
            at = pl.ds(pl.multiple_of(i * tile, tile), tile)
            out_ref[:, at] = weight_ref[at, :].T

    out_shape = [pltpu.VMEM((columns, rows), weight.dtype)]
    return call("transposed", kernel, 256 * rows * columns, [weight], out_shape, 4)[0]


def backward(weights, firsts, seconds, sums, jobs=(), held=None):
    width, size = weights[0].shape
    args, places = [], {}

    def add(array):
        if id(array) not in places:
            places[id(array)] = len(args)
            args.append(array)
        return places[id(array)]

    def add_all(arrays):
        return [array if isinstance(array, int) else (add(array),) for array in arrays]

    weight_at = [add(weight) for weight in weights]
    first_at = [add_all(pair) for pair in firsts]
    second_at = [(add_all(pair), add(back), add(pre)) for pair, back, pre in seconds]
    job_at = [(add_all(left), add_all(right)) for left, right, _, _ in jobs]
    sums_at = [add(array) for array in sums]
    count, backs, dpres = len(args) + (held is not None), len(firsts), len(seconds)

    def kernel(*refs):
        ins, outs = refs[:count], refs[count:]
        dpre_refs = outs[backs : backs + dpres]
        grad_sum_ref, dpre_sum_ref = outs[backs + dpres : backs + dpres + 2]
        job_refs, scratch = outs[backs + dpres + 2 :][: len(jobs)], outs[backs + dpres + 2 + len(jobs) :]

        def pick(ats):
            return [dpre_refs[at] if isinstance(at, int) else ins[at[0]] for at in ats]

        for k, sum_ref in enumerate((grad_sum_ref, dpre_sum_ref)):
            sum_ref[...] = ins[sums_at[k]][...] if sums else jnp.zeros(sum_ref.shape, f32)
        square_ref = None if sums else outs[backs + dpres + 2]
        for at, back_ref in zip(first_at, outs):
            first_back(pick(at), ins[weight_at[0]], back_ref, grad_sum_ref, square_ref)
        for (at, back, pre), dpre_ref in zip(second_at, dpre_refs):
            second_back(pick(at), ins[weight_at[1]], ins[back], ins[pre], dpre_ref, dpre_sum_ref)
        work = [
            (pick(left), pick(right), out_ref.at[index])
            for (left, right), out_ref, (_, _, _, index) in zip(job_at, job_refs, jobs)
        ]
        if work:
            outers(work, *scratch)

    out_shape = [shape((2 * pair[0].shape[0], size), f32) for pair in firsts]
    out_shape += [shape(pre.shape, bf16) for _, _, pre in seconds]
    out_shape += [shape((1, width), f32), shape((1, size), f32)] + [shape((1, width), f32)] * (not sums)
    in_specs, out_specs = [VMEM] * len(args), [VMEM] * len(out_shape)
    flops = 2 * sum(part.size for part in out_shape[: backs + dpres]) * width
    scratch, aliases = [], {}
    for left, right, lead, _ in jobs:
        columns = size if isinstance(right[-1], int) else right[0].shape[1]
        out_shape.append(shape((lead, left[0].shape[1], columns), bf16))
        out_specs.append(ANY)
        flops += 2 * out_shape[-1].size // lead * sum(part.shape[0] for part in left)
    if jobs:
        scratch = outer_scratch(max(size, width), max(part.shape[2] for part in out_shape[-len(jobs) :]))
    if held is not None:
        aliases = {len(args): backs + dpres + 2}
        args.append(held)
        in_specs.append(ANY)
    limit = 16 if jobs else 6
    outs = call("backward", kernel, flops, args, out_shape, limit, in_specs, out_specs, scratch, aliases)
    return outs[:backs], outs[backs : backs + dpres], outs[backs + dpres :]


def shards(inputs, targets, enc_weight, enc_bias, dec_weight, dec_bias):
    rows = inputs.shape[1]
    width = dec_weight.shape[3]
    layers, chips = lax.axis_size("layer"), lax.axis_size("feat") // 2
    layer = jnp.zeros((width,), f32) + lax.axis_index("layer").astype(f32)
    held, layer = lax.optimization_barrier((inputs[0], layer))
    inner, final = layer > 0.0, layer == layers - 1.0

    tokens = [(held, swapped(held))]
    pre, act, encoder, *decoders = prepared(tokens[0], enc_weight[0], dec_weight[0], enc_bias)
    pres, acts, sums = [pre], [act], [None] * chips

    def spread(j, mine, theirs):
        both = mine + swapped(theirs).astype(f32)
        later = both[:, width:].astype(bf16)
        sums[j] = both[:, :width], round_layers(later, 1)
        return later

    def run(j, *others):
        held, other = tokens[j]
        pre, act, mine, theirs = chunk((after(held, *others), other), encoder, enc_bias, decoders)
        pres.append(pre)
        acts.append(act)
        return mine, theirs

    def summed(j):
        here, later = sums[j]
        return here + jnp.where(inner, later.astype(f32), 0.0)

    order = list(range(1, chips)) + [0]
    total, done = None, acts[0]
    if chips > 1:
        held = after(from_below(tokens[0][0]), done)
        tokens.append((held, swapped(held)))
    for j in order:
        if j == 0:
            break
        mine, theirs = run(j, *([total] if j > 2 else [done]))
        if j == 1:
            first = decoded(after(acts[0], theirs), decoders)
            done = first[1]
        if j < chips - 1:
            theirs, held, done = lax.optimization_barrier((theirs, from_below(tokens[-1][0]), done))
            tokens.append((held, swapped(held)))
        if j == 2:
            total = summed(1)
        if j > 2:
            arrived = from_below(total.astype(bf16)).astype(f32)
            total = arrived + summed(j - 1)
            theirs = after(theirs, total)
        done = spread(j, mine, theirs)
        if j == 1:
            spread(0, *first)
    if chips < 3:
        total = summed(order[0])
    decoders_t = []
    for j in order[max(chips - 2, 1) :]:
        arrived = from_below(total.astype(bf16))
        if len(decoders_t) < len(decoders):
            decoders_t.append(transposed(after(decoders[len(decoders_t)], total)))
            arrived = after(arrived, decoders_t[-1])
        total = arrived.astype(f32) + summed(j)
    decoders_t += [transposed(decoder) for decoder in decoders[len(decoders_t) :]]

    grad = (total + dec_bias[0] - targets[0].astype(f32)).astype(bf16)

    here, later, backs, dpres, acc = [(grad, swapped(grad))], [], [], [], []
    (back,), _, (*acc, squares) = backward(decoders_t, here, [], [])
    done, dec_grad, pending = back, None, []
    entries = layers * lax.axis_size("feat") * rows * width
    hops = [[(from_below, k) for k in range(1, chips)], [(round_layers, k) for k in range(1, layers)]]
    for j in range(chips):
        if j < chips - 1:
            held = done = after(from_below(here[j][0]), done)
        ahead = after(round_layers(here[j][0], -1), done)
        ahead = jnp.where(final, jnp.zeros_like(ahead), ahead)
        if pending:
            squares = sum(after(block, ahead) for block in pending) + squares
            held, ahead = lax.optimization_barrier((held, ahead, squares))[:2]
        if j < chips - 1:
            here.append((held, swapped(held)))
        later.append((ahead, swapped(ahead)))
        pending = []
        if hops and j < chips - 1:
            pending = [move(squares, distance) for move, distance in hops.pop(0)]
        if j == chips - 1:
            break
        jobs = []
        if j == chips - 2:
            jobs = [(acts, [part for pair in here for part in pair], 2, 0)]
        second = later[j], back, pres[j]
        if jobs:
            (back,), _, (*acc, dec_grad) = backward(decoders_t, [here[j + 1]], [], acc[:2], jobs)
            pair, *second = second
            second = (after(pair[0], back), pair[1]), *second
            _, (dpre,), acc = backward(decoders_t, [], [second], acc[:2])
            done = back
        else:
            (back,), (dpre,), acc = backward(decoders_t, [here[j + 1]], [second], acc[:2])
            done = dpre
        dpres.append(dpre)

    flat = [part for pair in tokens for part in pair]
    jobs = [(acts, [part for pair in later for part in pair], 2, 1), (flat, [*dpres, 0], 1, 0)]
    _, _, (grad_sum, dpre_sum, dec_grad, enc_grad) = backward(
        decoders_t, [], [(later[-1], back, pres[-1])], acc[:2], jobs, dec_grad
    )
    for moves in hops:
        squares = sum(move(squares, distance) for move, distance in moves) + squares
    return (jnp.sum(squares / entries), enc_grad, dpre_sum, dec_grad[None], grad_sum)


def solution(mesh):
    return jax.shard_map(
        shards,
        mesh=mesh,
        in_specs=(
            P("layer", "feat", None),
            P("layer", "feat", None),
            P("layer", None, "feat"),
            P("layer", "feat"),
            P("layer", None, "feat", None),
            P("layer", None),
        ),
        out_specs=(
            P(),
            P("layer", None, "feat"),
            P("layer", "feat"),
            P("layer", None, "feat", None),
            P("layer", None),
        ),
        check_vma=False,
    )
```
